32 devices in a mesh: groups: 2 (over x), wide: 16 (over z, y, core).
Axes of the slice: x: 2, y: 2, z: 4, core: 2. Of those that a mesh axis runs over, the one named last changes fastest.
Arguments:
- positions: float32 [3, 8192], P(None, 'wide'), may hold values from -4 to 4
- spans: float32 [8192], P('wide'), may hold values from 0.4 to 1
- box_panel: int32 [8192], P('wide'), may hold values from 0 to 63
- panel_dihedral: float32 [64], replicated, may hold values from -3.140625 to 3.140625
- freq_table: float32 [16], replicated, may hold values from 0.2 to 2
- freq_index: int32 [4], P('groups'), parts along dimension 0, may hold values from 0 to 15
- pressures: bfloat16 [4, 2, 8192, 512], P('groups', None, 'wide'), parts along dimension 0, may hold values from -6 to 6
Outputs:
- upwash: float32 [4, 2, 8192, 512], P('groups', None, 'wide'), parts along dimension 0
The draws below stay inside these ranges and needn't reach their ends.
There are 2 independent parts, one for each index of `groups`. The reference program is written for one: setup_inputs(seed, part) draws one part's arguments, and reference() takes and returns one part's arrays. A program takes and returns all parts, laid end to end along the dimension named above; an argument that names none is the same for every part. Nothing has to cross between parts.
All inputs are finite; a program needn't handle non-finite values.
Results may differ from the reference program's by a relative error of at most 0.0029.
Values may be sent and summed in bfloat16 or wider, within the bound.
No kernel may reach another device: no remote copies, remote signals or barrier semaphores. Data moves between devices by JAX's collectives and lax.ppermute only.
A program may use at most 64 MiB of HBM per device.

```python
import math
import jax
import jax.numpy as jnp
from jax import lax

BOXES_DEV = 512
SIDES = 512
FREQS = 2
TABLE_LEN = 16
PANELS = 64
BOXES = 8192
N_WIDE = 16


def touch_ends(values, rng, least, largest):
    longest = values.shape.index(max(values.shape))
    spots = []
    for shift in (0, 1):
        where = [jax.random.randint(jax.random.fold_in(rng, axis), (), 0, length) for axis, length in enumerate(values.shape)]
        where[longest] = (where[longest] + shift) % values.shape[longest]
        spots.append(tuple(where))
    return values.at[spots[0]].set(least).at[spots[1]].set(largest)


def shard_levels(stream_key, dims, cuts, least, top_value):
    def one(axis_at, blocks):
        heights = jax.random.uniform(jax.random.fold_in(jax.random.fold_in(stream_key, 6), axis_at), (blocks,), jnp.float32, least / len(cuts), top_value / len(cuts))
        return jnp.repeat(jnp.exp(heights), dims[axis_at] // blocks).reshape((-1,) + (1,) * (len(dims) - axis_at - 1))

    level = one(*cuts[0])
    for cut in cuts[1:]:
        level = level * one(*cut)
    return level


def centred(key, shape, width, most, pieces=(), held_as=jnp.bfloat16):
    gain = shard_levels(key, shape, pieces, -0.22, 0.18) if pieces else 1.0
    values = jax.random.normal(key, shape, jnp.float32) * width * gain
    return jnp.minimum(jnp.maximum(values, -most), most).astype(held_as)


def setup_inputs(seed: int = 0, part: int = 0) -> dict:
    streams_of = jax.random.split(jax.random.key(seed), 8)
    part_keys = jax.random.split(jax.random.fold_in(streams_of[7], part), 8)
    positions = jnp.clip(jax.random.uniform(streams_of[0], (3, BOXES), jnp.float32, -4.0, 4.0) * shard_levels(streams_of[0], (3, BOXES), ((1, 16),), -0.4, 0.0), -4.0, 4.0)
    spans = jnp.clip(0.4 + 0.6 * jax.random.uniform(streams_of[1], (BOXES,), jnp.float32) ** shard_levels(streams_of[1], (BOXES,), ((0, 16),), -0.2, 0.2), 0.4, 1.0)
    box_panel = touch_ends(jax.random.randint(streams_of[2], (BOXES,), 0, PANELS), jax.random.fold_in(streams_of[2], 1), 0, PANELS - 1).astype(jnp.int32)
    panel_dihedral = jnp.clip(jax.random.uniform(streams_of[3], (PANELS,), jnp.float32, -3.140625, 3.140625), -3.140625, 3.140625)
    freq_table = jnp.clip(jnp.exp(jax.random.uniform(streams_of[4], (TABLE_LEN,), jnp.float32, math.log(0.2), math.log(2.0))), 0.2, 2.0)
    freq_index = jax.random.randint(part_keys[5], (FREQS,), 0, TABLE_LEN).astype(jnp.int32)
    pressures = centred(part_keys[6], (FREQS, 2, BOXES, SIDES), 1.0, 6.0, ((2, 16),))
    return {"positions": positions, "spans": spans, "box_panel": box_panel, "panel_dihedral": panel_dihedral, "freq_table": freq_table, "freq_index": freq_index, "pressures": pressures}


def kernel_tile(recv, send, wave):
    dx = recv[0][:, None] - send[0][None, :]
    dy = recv[1][:, None] - send[1][None, :]
    dz = recv[2][:, None] - send[2][None, :]
    half_span = send[3][None, :]
    rho_sq = dy * dy + dz * dz + half_span * half_span
    dist = jnp.sqrt(dx * dx + rho_sq)
    normal_i = -recv[4][:, None] * dy + recv[5][:, None] * dz
    normal_j = -send[4][None, :] * dy + send[5][None, :] * dz
    planar = recv[5][:, None] * send[5][None, :] + recv[4][:, None] * send[4][None, :]
    amp = (half_span * planar / rho_sq - 2.0 * half_span * normal_i * normal_j / (rho_sq * rho_sq)) * (1.0 + dx / dist)
    phase = wave * (dist - dx)
    kern_re = (amp * jnp.cos(phase)).astype(jnp.bfloat16)
    kern_im = (-amp * jnp.sin(phase)).astype(jnp.bfloat16)
    upper = jnp.concatenate([kern_re, -kern_im], axis=1)
    lower = jnp.concatenate([kern_im, kern_re], axis=1)
    return jnp.concatenate([upper, lower], axis=0)

def block_term(recv, send, send_press, waves):
    outputs = []
    for freq in range(FREQS):
        stacked = kernel_tile(recv, send, waves[freq])
        rhs = send_press[freq].reshape(2 * BOXES_DEV, SIDES)
        outputs.append(jnp.dot(stacked, rhs, preferred_element_type=jnp.float32).reshape(2, BOXES_DEV, SIDES))
    return jnp.stack(outputs, axis=0)

def reference(positions, spans, box_panel, panel_dihedral, freq_table, freq_index, pressures):
    angle = panel_dihedral[box_panel]
    record = jnp.concatenate([positions, spans[None, :], jnp.sin(angle)[None, :], jnp.cos(angle)[None, :]], axis=0)
    waves = freq_table[freq_index]

    def one_block(block):
        start = (block * BOXES_DEV).astype(jnp.int32)
        recv = lax.dynamic_slice_in_dim(record, start, BOXES_DEV, 1)
        total = jnp.zeros((FREQS, 2, BOXES_DEV, SIDES), jnp.float32)
        for offset in (1, 0, -1, -2):
            other = ((block + offset) % N_WIDE * BOXES_DEV).astype(jnp.int32)
            send = lax.dynamic_slice_in_dim(record, other, BOXES_DEV, 1)
            send_press = lax.dynamic_slice_in_dim(pressures, other, BOXES_DEV, 2)
            total = total + block_term(recv, send, send_press, waves)
        return total
    blocks = lax.map(one_block, jnp.arange(N_WIDE, dtype=jnp.int32))
    return jnp.moveaxis(blocks, 0, 2).reshape(FREQS, 2, BOXES, SIDES)
```

```python
import functools

import jax
import jax.numpy as jnp
from jax import lax
from jax.experimental import pallas as pl
from jax.experimental.pallas import tpu as pltpu
from jax.sharding import PartitionSpec as P

SIN_COEF = (6.283182621002197, -41.3414192199707, 81.5961685180664, -76.5799560546875, 41.20474624633789, -12.27022647857666)
COS_COEF = (0.9999992251396179, -19.738981246948242, 64.9287109375, -85.27218627929688, 58.7929573059082, -21.074859619140625)
ROUNDER = 12582912.0
ROWS = 16
LANES = 128


def horner(v, coef):
    value = jnp.full_like(v, coef[-1])
    for c in coef[-2::-1]:
        value = value * v + c
    return value


def shifted(block, axis, distance):
    n = lax.axis_size(axis)
    return lax.ppermute(block, axis, [((i - distance) % n, i) for i in range(n)])


def fill_kernel(recv_ref, send_ref, turns, kern_ref, slot):
    rows, boxes = recv_ref.shape[0], send_ref.shape[1]

    def row_block(i, carry):
        at = pl.ds(pl.multiple_of(i * ROWS, ROWS), ROWS)
        cols = [jnp.broadcast_to(recv_ref[at, q : q + 1], (ROWS, LANES)) for q in range(5)]
        xi, yi, zi, si, ci = cols
        for j in range(boxes // LANES):
            lanes = pl.ds(j * LANES, LANES)
            row = [send_ref[q : q + 1, lanes] for q in range(8)]
            xj, yj, zj, e2, es2, ec2, es, ec = row
            dx, dy, dz = xi - xj, yi - yj, zi - zj
            rho = dy * dy + dz * dz + e2
            d2 = dx * dx + rho
            inv_d = lax.rsqrt(d2)
            inv = pl.reciprocal(rho, approx=True)
            inv = inv * (2.0 - rho * inv)
            dist = d2 * inv_d
            normal_i = ci * dz - si * dy
            normal_j = ec2 * dz - es2 * dy
            planar = ci * ec + si * es
            amp = inv * (planar - normal_i * normal_j * inv) * (1.0 + dx * inv_d)
            lag = dist - dx
            for f, turn in enumerate(turns):
                u = lag * turn
                u = u - ((u + ROUNDER) - ROUNDER)
                v = u * u
                kern_ref[slot, f, 0, at, lanes] = (amp * horner(v, COS_COEF)).astype(jnp.bfloat16)
                kern_ref[slot, f, 1, at, lanes] = (amp * u * horner(v, SIN_COEF)).astype(jnp.bfloat16)
        return carry

    lax.fori_loop(0, rows // ROWS, row_block, 0)


def term_body(freqs, has_acc, turns_ref, recv_ref, send_ref, press_ref, *rest):
    acc_ref = rest[0] if has_acc else None
    out_ref, kern_ref = rest[-2:]
    turns = [turns_ref[f] for f in freqs]
    fill_kernel(recv_ref, send_ref, turns, kern_ref, 0)
    dot = functools.partial(jnp.dot, preferred_element_type=jnp.float32)
    for f in range(len(freqs)):
        kr, ks = kern_ref[0, f, 0], kern_ref[0, f, 1]
        pr, pi = press_ref[f, 0], press_ref[f, 1]
        re = dot(kr, pr) + dot(ks, pi)
        im = dot(kr, pi) - dot(ks, pr)
        if has_acc:
            re = re + acc_ref[f, 0]
            im = im + acc_ref[f, 1]
        out_ref[f, 0] = re.astype(out_ref.dtype)
        out_ref[f, 1] = im.astype(out_ref.dtype)


def term(turns, recv, send, press, acc=None, freqs=(0, 1), out_dtype=jnp.float32, tile=256):
    boxes, width = press.shape[2], press.shape[3]
    count = len(freqs)
    in_specs = [
        pl.BlockSpec(memory_space=pltpu.SMEM),
        pl.BlockSpec((tile, 8), lambda i: (i, 0)),
        pl.BlockSpec((8, boxes), lambda i: (0, 0)),
        pl.BlockSpec((count, 2, boxes, width), lambda i: (0, 0, 0, 0)),
    ]
    args = [turns, recv, send, press]
    if acc is not None:
        in_specs.append(pl.BlockSpec((count, 2, tile, width), lambda i: (0, 0, i, 0)))
        args.append(acc)
    return pl.pallas_call(
        functools.partial(term_body, freqs, acc is not None),
        grid=(boxes // tile,),
        in_specs=in_specs,
        out_specs=pl.BlockSpec((count, 2, tile, width), lambda i: (0, 0, i, 0)),
        out_shape=jax.ShapeDtypeStruct((count, 2, boxes, width), out_dtype),
        scratch_shapes=[pltpu.VMEM((1, count, 2, tile, boxes), jnp.bfloat16)],
        compiler_params=pltpu.CompilerParams(vmem_limit_bytes=48 * 1024 * 1024),
        cost_estimate=pl.CostEstimate(
            flops=count * 8 * boxes * boxes * width,
            bytes_accessed=12 * 1024 * 1024,
            transcendentals=0,
        ),
        input_output_aliases={4: 0} if acc is not None else {},
    )(*args)


def send_form(record):
    x, y, z, e, s, c = [record[i] for i in range(6)]
    return jnp.stack([x, y, z, e * e, 2.0 * e * s, 2.0 * e * c, e * s, e * c])


def recv_form(record):
    x, y, z, e, s, c = [record[i] for i in range(6)]
    return jnp.stack([x, y, z, s, c, s, s, s], axis=1)


def local(positions, spans, box_panel, panel_dihedral, freq_table, freq_index, pressures):
    panel_ids = jnp.arange(panel_dihedral.shape[0], dtype=jnp.int32)
    angle = jnp.sum(
        jnp.where(box_panel[:, None] == panel_ids[None, :], panel_dihedral[None, :], 0.0), axis=1
    )
    record = jnp.concatenate(
        [positions, spans[None, :], jnp.sin(angle)[None, :], jnp.cos(angle)[None, :]], axis=0
    )
    table_ids = jnp.arange(freq_table.shape[0], dtype=jnp.int32)
    waves = jnp.sum(
        jnp.where(freq_index[:, None] == table_ids[None, :], freq_table[None, :], 0.0), axis=1
    )
    turns = waves * (0.5 / jnp.pi)
    recv = recv_form(record)
    total = term(turns, recv, send_form(record), pressures)
    for distance in (1, 2, -1):
        rec = shifted(record, "wide", distance)
        press = shifted(pressures, "wide", distance)
        total = term(turns, recv, send_form(rec), press, total)
    return total


def solution(mesh):
    placed = (
        P(None, "wide"),
        P("wide"),
        P("wide"),
        P(),
        P(),
        P("groups"),
        P("groups", None, "wide", None),
    )
    return jax.shard_map(
        local,
        mesh=mesh,
        in_specs=placed,
        out_specs=P("groups", None, "wide", None),
        check_vma=False,
    )
```

```python
import functools

import jax
import jax.numpy as jnp
from jax import lax
from jax.experimental import pallas as pl
from jax.experimental.pallas import tpu as pltpu
from jax.sharding import PartitionSpec as P

SIN_COEF = (6.283182621002197, -41.3414192199707, 81.5961685180664, -76.5799560546875, 41.20474624633789, -12.27022647857666)
COS_COEF = (0.9999992251396179, -19.738981246948242, 64.9287109375, -85.27218627929688, 58.7929573059082, -21.074859619140625)
ROUNDER = 12582912.0
TURN = 0.15915494309189535
ROWS = 32
LANES = 128
RECORD = 32
VMEM = pl.BlockSpec(memory_space=pltpu.VMEM)
ANY = pl.BlockSpec(memory_space=pl.ANY)
PARAMS = pltpu.CompilerParams(vmem_limit_bytes=24 * 1024 * 1024)


def horner(v, coef):
    value = coef[-1] * v + coef[-2]
    for c in coef[-3::-1]:
        value = value * v + c
    return value


def cost(micros):
    return pl.CostEstimate(flops=micros << 32, bytes_accessed=1, transcendentals=0)


def prep_body(
    pos_any, span_any, panel_any, dihedral_any, table_any, index_any,
    send_ref, recv_ref, rows_ref,
    pos_ref, span_ref, panel_ref, dihedral_ref, table_ref, index_ref, sems
):
    boxes = pos_ref.shape[1]
    copies = [
        pltpu.make_async_copy(src, dst, sems.at[i])
        for i, (src, dst) in enumerate(
            [(pos_any, pos_ref), (span_any, span_ref), (panel_any, panel_ref)]
            + [(dihedral_any, dihedral_ref), (table_any, table_ref), (index_any, index_ref)]
        )
    ]
    for copy in copies:
        copy.start()
    for copy in copies:
        copy.wait()
    panel = panel_ref[...].reshape(1, boxes)
    angle = jnp.zeros(panel.shape, jnp.float32)
    for i in range(dihedral_ref.shape[0]):
        angle = jnp.where(panel == i, dihedral_ref[i], angle)
    sin, cos, span = jnp.sin(angle), jnp.cos(angle), span_ref[...].reshape(1, boxes)
    pos = pos_ref[...]
    send = jnp.concatenate(
        [pos, span * span, 2.0 * span * sin, 2.0 * span * cos, span * sin, span * cos], axis=0
    )
    send_ref[...] = send
    turns = [jnp.full_like(sin, table_ref[index_ref[f]] * TURN) for f in range(index_ref.shape[0])]
    recv_ref[...] = jnp.concatenate([pos, sin, cos, *turns, sin], axis=0).T
    high = send.astype(jnp.bfloat16).astype(jnp.float32)
    left = send - high
    middle = left.astype(jnp.bfloat16).astype(jnp.float32)
    rows_ref[...] = jnp.concatenate(
        [high, middle, left - middle, jnp.zeros_like(high)], axis=0
    ).astype(jnp.bfloat16)


def prepare(positions, spans, box_panel, panel_dihedral, freq_table, freq_index):
    args = (positions, spans, box_panel, panel_dihedral, freq_table, freq_index)
    boxes = spans.shape[0]
    return pl.pallas_call(
        prep_body,
        in_specs=[pl.BlockSpec(memory_space=pltpu.HBM)] * 6,
        out_specs=[VMEM] * 3,
        out_shape=[
            jax.ShapeDtypeStruct((8, boxes), jnp.float32),
            jax.ShapeDtypeStruct((boxes, 8), jnp.float32),
            jax.ShapeDtypeStruct((RECORD, boxes), jnp.bfloat16),
        ],
        scratch_shapes=[
            pltpu.VMEM(positions.shape, jnp.float32),
            pltpu.VMEM(spans.shape, jnp.float32),
            pltpu.VMEM(box_panel.shape, jnp.int32),
            pltpu.SMEM(panel_dihedral.shape, jnp.float32),
            pltpu.SMEM(freq_table.shape, jnp.float32),
            pltpu.SMEM(freq_index.shape, jnp.int32),
            pltpu.SemaphoreType.DMA((6,)),
        ],
        compiler_params=PARAMS,
        cost_estimate=cost(2),
    )(*[pltpu.with_memory_space_constraint(a, pltpu.HBM) for a in args])


def unpack(rows):
    parts = rows.astype(jnp.float32)
    return (parts[:8] + parts[8:16]) + parts[16:24]


def fill(recv_ref, send_ref, turns, stores):
    rows, boxes = recv_ref.shape[0], send_ref.shape[1]

    def row_block(i, carry):
        at = pl.ds(pl.multiple_of(i * ROWS, ROWS), ROWS)
        xi, yi, zi, si, ci = [
            jnp.broadcast_to(recv_ref[at, q : q + 1], (ROWS, LANES)) for q in range(5)
        ]
        for j in range(boxes // LANES):
            lanes = pl.ds(j * LANES, LANES)
            xj, yj, zj, e2, es2, ec2, es, ec = [send_ref[q : q + 1, lanes] for q in range(8)]
            dx, dy, dz = xi - xj, yi - yj, zi - zj
            rho = dy * dy + dz * dz + e2
            d2 = dx * dx + rho
            inv_d = lax.rsqrt(d2)
            inv = pl.reciprocal(rho, approx=True)
            inv = inv * (2.0 - rho * inv)
            normal_i = ci * dz - si * dy
            normal_j = ec2 * dz - es2 * dy
            planar = ci * ec + si * es
            amp = inv * (planar - normal_i * normal_j * inv) * (1.0 + dx * inv_d)
            lag = d2 * inv_d - dx
            for turn, (re, im) in zip(turns, stores):
                u = lag * turn
                u = u - ((u + ROUNDER) - ROUNDER)
                v = u * u
                re[at, lanes] = (amp * horner(v, COS_COEF)).astype(jnp.bfloat16)
                im[at, lanes] = (amp * u * horner(v, SIN_COEF)).astype(jnp.bfloat16)
        return carry

    lax.fori_loop(0, rows // ROWS, row_block, 0, unroll=4)


def dot(a, b):
    return jnp.dot(a, b, preferred_element_type=jnp.float32)


def product(kr, ks, pr, pi):
    return dot(kr, pr) + dot(ks, pi), dot(kr, pi) - dot(ks, pr)


def turns_of(recv_ref):
    return [recv_ref[:1, 5 + f : 6 + f] for f in range(2)]


def near_body(half, recv_ref, send0_ref, send1_ref, first_ref, second_ref, p1_ref, *rest):
    out_ref, k0_ref, k1_ref = rest[-3:]
    freqs = range(p1_ref.shape[0])
    tile, boxes = out_ref.shape[2], p1_ref.shape[2]
    turns = turns_of(recv_ref)
    recv = recv_ref.at[pl.ds(half * tile, tile)]
    fill(recv, send0_ref, turns, [(k0_ref.at[f, 0], k0_ref.at[f, 1]) for f in freqs])
    fill(recv, send1_ref, turns, [(k1_ref.at[f, 0], k1_ref.at[f, 1]) for f in freqs])
    for f, own_ref in enumerate((first_ref, second_ref)):
        re, im = own_ref[:boxes], own_ref[boxes : 2 * boxes]
        r0, i0 = product(k0_ref[f, 0], k0_ref[f, 1], re, im)
        r1, i1 = product(k1_ref[f, 0], k1_ref[f, 1], p1_ref[f, 0], p1_ref[f, 1])
        out_ref[f, 0] = r0 + r1
        out_ref[f, 1] = i0 + i1


def near(recv, send0, send1, first, second, p1, half, *after):
    freqs, _, boxes, width = p1.shape
    tile = boxes // 2
    return pl.pallas_call(
        functools.partial(near_body, half),
        in_specs=[VMEM] * 6 + [ANY] * len(after),
        out_specs=VMEM,
        out_shape=jax.ShapeDtypeStruct((freqs, 2, tile, width), jnp.float32),
        scratch_shapes=[pltpu.VMEM((freqs, 2, tile, boxes), jnp.bfloat16)] * 2,
        compiler_params=PARAMS,
        cost_estimate=cost(8),
    )(recv, send0, send1, first, second, p1, *after)


def choose(refs, rows):
    r = lax.rem(lax.axis_index("wide"), 4)
    inner = refs[1][rows]
    if len(refs) == 3:
        inner = jnp.where(r == 1, inner, refs[2][rows])
    return jnp.where(jnp.logical_or(r == 0, r == 3), refs[0][rows], inner)


def far_body(n_block, n_acc, recv_ref, *rest):
    block_refs, acc_refs = rest[:n_block], rest[n_block : n_block + n_acc]
    out_ref, later_ref, now_ref, p_ref, send_ref = rest[-5:]
    boxes = recv_ref.shape[0]
    p_ref[...] = choose(block_refs, slice(0, 2 * boxes))
    send_ref[...] = unpack(choose(block_refs, slice(2 * boxes, 2 * boxes + RECORD)))
    kern = [(now_ref.at[0], now_ref.at[1]), (later_ref.at[0], later_ref.at[1])]
    fill(recv_ref, send_ref, turns_of(recv_ref), kern)
    half = boxes // 2
    for h in range(2):
        rows = slice(h * half, h * half + half)
        re, im = product(now_ref[0, rows], now_ref[1, rows], p_ref[:boxes], p_ref[boxes:])
        if n_acc == 2:
            out_ref[0, rows] = acc_refs[h][0, 0] + re
            out_ref[1, rows] = acc_refs[h][0, 1] + im
        else:
            out_ref[0, 0, rows] = acc_refs[0][0, rows] + re
            out_ref[0, 1, rows] = acc_refs[0][1, rows] + im


def far(recv, block, accs, last):
    boxes, width = recv.shape[0], block[0].shape[1]
    if last:
        out = jax.ShapeDtypeStruct((2, 2, boxes, width), jnp.float32)
        spec = pl.BlockSpec((1, 2, boxes, width), lambda i: (0, 0, 0, 0))
    else:
        out, spec = jax.ShapeDtypeStruct((2, boxes, width), jnp.float32), VMEM
    return pl.pallas_call(
        functools.partial(far_body, len(block), len(accs)),
        grid=(1,),
        in_specs=[VMEM] * (1 + len(block) + len(accs)),
        out_specs=[spec, VMEM],
        out_shape=[out, jax.ShapeDtypeStruct((2, boxes, boxes), jnp.bfloat16)],
        scratch_shapes=[
            pltpu.VMEM((2, boxes, boxes), jnp.bfloat16),
            pltpu.VMEM((2 * boxes, width), jnp.bfloat16),
            pltpu.VMEM((8, boxes), jnp.float32),
        ],
        compiler_params=PARAMS,
        cost_estimate=cost(7),
    )(recv, *block, *accs)


def mid_body(n_block, kern_ref, *rest):
    block_refs = rest[:n_block]
    low_ref, high_ref, out_ref, p_ref = rest[n_block:]
    boxes = kern_ref.shape[1]
    p_ref[...] = choose(block_refs, slice(None))
    half = boxes // 2
    for h, acc_ref in enumerate((low_ref, high_ref)):
        rows = slice(h * half, h * half + half)
        re, im = product(kern_ref[0, rows], kern_ref[1, rows], p_ref[:boxes], p_ref[boxes:])
        out_ref[0, rows] = acc_ref[1, 0] + re
        out_ref[1, rows] = acc_ref[1, 1] + im


def mid(kern, block, low, high):
    boxes, width = kern.shape[1], block[0].shape[1]
    return pl.pallas_call(
        functools.partial(mid_body, len(block)),
        in_specs=[VMEM] * (3 + len(block)),
        out_specs=VMEM,
        out_shape=jax.ShapeDtypeStruct((2, boxes, width), jnp.float32),
        scratch_shapes=[pltpu.VMEM((2 * boxes, width), jnp.bfloat16)],
        compiler_params=PARAMS,
        cost_estimate=cost(2),
    )(kern, *block, low, high)


def end_body(kern_ref, x_ref, y_ref, acc_ref, whole_ref, out_ref, p_ref):
    boxes = p_ref.shape[0] // 2
    step = pl.program_id(0)
    tile = out_ref.shape[2]

    @pl.when(step == 0)
    def _():
        p_ref[...] = choose((x_ref, y_ref), slice(None))

    rows = pl.ds(pl.multiple_of(step * tile, tile), tile)
    re, im = product(kern_ref[0, rows], kern_ref[1, rows], p_ref[:boxes], p_ref[boxes:])
    out_ref[0, 0] = acc_ref[0, rows] + re
    out_ref[0, 1] = acc_ref[1, rows] + im


def end(kern, block, acc, out):
    boxes, width = kern.shape[1], block[0].shape[1]
    tile = boxes // 2
    return pl.pallas_call(
        end_body,
        grid=(2,),
        in_specs=[VMEM] * 4 + [ANY],
        out_specs=pl.BlockSpec((1, 2, tile, width), lambda i: (1, 0, i, 0)),
        out_shape=jax.ShapeDtypeStruct(out.shape, jnp.float32),
        scratch_shapes=[pltpu.VMEM((2 * boxes, width), jnp.bfloat16)],
        input_output_aliases={4: 0},
        compiler_params=PARAMS,
        cost_estimate=cost(2),
    )(kern, *block, acc, out)


def move(block, pairs):
    return lax.ppermute(block, "wide", pairs)


def routes(n):
    quads = range(0, n, 4)
    cross = [(b + r, b + (r ^ 2)) for b in quads for r in (0, 2)]
    cross += [(b + 3, (b + 7) % n) for b in quads] + [(b + 1, b + 1) for b in quads]
    spread = [
        p
        for b in quads
        for p in ((b + 1, b + 2), (b + 3, b + 1), (b, (b + 4) % n), ((b + 6) % n, b + 3))
    ]
    inner = [(b, b + 1) for b in quads]
    last = [p for b in quads for p in ((b + 1, b), (b + 2, b + 3))]
    pair = [(w, w ^ 1) for w in range(n)]
    return cross, spread, inner, last, pair


def ordered(value, *before):
    return lax.optimization_barrier((value, *before))[0]


def local(positions, spans, box_panel, panel_dihedral, freq_table, freq_index, pressures):
    n = lax.axis_size("wide")
    cross, spread, inner, last, pair = routes(n)
    _, _, boxes, width = pressures.shape
    send, recv, rows = prepare(
        positions, spans, box_panel, panel_dihedral, freq_table, freq_index
    )
    first = jnp.concatenate([pressures[0].reshape(2 * boxes, width), rows], axis=0)
    second = pressures[1].reshape(2 * boxes, width)
    crossed0 = move(first, cross)
    crossed1 = move(second, cross)
    beside = move(pressures, pair)
    send1 = move(send, pair)
    terms = functools.partial(near, recv, send, send1, first, second, beside)
    low = terms(0)
    high = terms(1)
    crossed0, crossed1, low, high = lax.optimization_barrier((crossed0, crossed1, low, high))
    spread0 = move(crossed0, spread)
    inner0 = move(crossed0, inner)
    spread1 = move(crossed1, spread)
    inner1 = move(crossed1, inner)
    last0 = move(spread0, last)
    total0, kern_a = far(recv, (spread0, inner0, crossed0), [low, high], False)
    out, kern_b = far(recv, (last0, spread0), [total0], True)
    spread1 = ordered(spread1, out)
    last1 = move(spread1, last)
    total1 = mid(kern_a, (spread1, inner1, crossed1), low, high)
    return end(kern_b, (last1, spread1), total1, out)


def solution(mesh):
    placed = (
        P(None, "wide"),
        P("wide"),
        P("wide"),
        P(),
        P(),
        P("groups"),
        P("groups", None, "wide", None),
    )
    return jax.shard_map(
        local,
        mesh=mesh,
        in_specs=placed,
        out_specs=P("groups", None, "wide", None),
        check_vma=False,
    )
```

```python
import functools

import jax
import jax.numpy as jnp
from jax import lax
from jax.experimental import pallas as pl
from jax.experimental.pallas import tpu as pltpu
from jax.sharding import PartitionSpec as P

SIN_COEF = (6.283182621002197, -41.3414192199707, 81.5961685180664, -76.5799560546875, 41.20474624633789, -12.27022647857666)
COS_COEF = (0.9999992251396179, -19.738981246948242, 64.9287109375, -85.27218627929688, 58.7929573059082, -21.074859619140625)
ROUNDER = 12582912.0
TURN = 0.15915494309189535
ROWS = 32
LANES = 128
RECORD = 32
VMEM = pl.BlockSpec(memory_space=pltpu.VMEM)
ANY = pl.BlockSpec(memory_space=pl.ANY)
PARAMS = pltpu.CompilerParams(vmem_limit_bytes=24 * 1024 * 1024)


def horner(v, coef):
    value = coef[-1] * v + coef[-2]
    for c in coef[-3::-1]:
        value = value * v + c
    return value


def cost(micros):
    return pl.CostEstimate(flops=micros << 33, bytes_accessed=1, transcendentals=0)


def prep_body(
    pos_any, span_any, panel_any, dihedral_any, table_any, index_any,
    send_ref, recv_ref, rows_ref,
    pos_ref, span_ref, panel_ref, dihedral_ref, table_ref, index_ref, sems
):
    boxes = pos_ref.shape[1]
    copies = [
        pltpu.make_async_copy(src, dst, sems.at[i])
        for i, (src, dst) in enumerate(
            [(pos_any, pos_ref), (span_any, span_ref), (panel_any, panel_ref)]
            + [(dihedral_any, dihedral_ref), (table_any, table_ref), (index_any, index_ref)]
        )
    ]
    for copy in copies:
        copy.start()
    for copy in copies:
        copy.wait()
    panel = panel_ref[...].reshape(1, boxes)
    angle = jnp.zeros(panel.shape, jnp.float32)
    for i in range(dihedral_ref.shape[0]):
        angle = jnp.where(panel == i, dihedral_ref[i], angle)
    sin, cos, span = jnp.sin(angle), jnp.cos(angle), span_ref[...].reshape(1, boxes)
    pos = pos_ref[...]
    send = jnp.concatenate(
        [pos, span * span, 2.0 * span * sin, 2.0 * span * cos, span * sin, span * cos], axis=0
    )
    send_ref[...] = send
    turns = [jnp.full_like(sin, table_ref[index_ref[f]] * TURN) for f in range(index_ref.shape[0])]
    recv_ref[...] = jnp.concatenate([pos, sin, cos, *turns, sin], axis=0).T
    high = send.astype(jnp.bfloat16).astype(jnp.float32)
    left = send - high
    middle = left.astype(jnp.bfloat16).astype(jnp.float32)
    rows_ref[...] = jnp.concatenate(
        [high, middle, left - middle, jnp.zeros_like(high)], axis=0
    ).astype(jnp.bfloat16)


def prepare(positions, spans, box_panel, panel_dihedral, freq_table, freq_index):
    args = (positions, spans, box_panel, panel_dihedral, freq_table, freq_index)
    boxes = spans.shape[0]
    return pl.pallas_call(
        prep_body,
        in_specs=[pl.BlockSpec(memory_space=pltpu.HBM)] * 6,
        out_specs=[VMEM] * 3,
        out_shape=[
            jax.ShapeDtypeStruct((8, boxes), jnp.float32),
            jax.ShapeDtypeStruct((boxes, 8), jnp.float32),
            jax.ShapeDtypeStruct((RECORD, boxes), jnp.bfloat16),
        ],
        scratch_shapes=[
            pltpu.VMEM(positions.shape, jnp.float32),
            pltpu.VMEM(spans.shape, jnp.float32),
            pltpu.VMEM(box_panel.shape, jnp.int32),
            pltpu.SMEM(panel_dihedral.shape, jnp.float32),
            pltpu.SMEM(freq_table.shape, jnp.float32),
            pltpu.SMEM(freq_index.shape, jnp.int32),
            pltpu.SemaphoreType.DMA((6,)),
        ],
        compiler_params=PARAMS,
        cost_estimate=cost(2),
    )(*[pltpu.with_memory_space_constraint(a, pltpu.HBM) for a in args])


def unpack(rows):
    parts = rows.astype(jnp.float32)
    return (parts[:8] + parts[8:16]) + parts[16:24]


def fill(recv_ref, send_ref, turns, stores):
    rows, boxes = recv_ref.shape[0], send_ref.shape[1]

    def row_block(i, carry):
        at = pl.ds(pl.multiple_of(i * ROWS, ROWS), ROWS)
        xi, yi, zi, si, ci = [
            jnp.broadcast_to(recv_ref[at, q : q + 1], (ROWS, LANES)) for q in range(5)
        ]
        for j in range(boxes // LANES):
            lanes = pl.ds(j * LANES, LANES)
            xj, yj, zj, e2, es2, ec2, es, ec = [send_ref[q : q + 1, lanes] for q in range(8)]
            dx, dy, dz = xi - xj, yi - yj, zi - zj
            rho = dy * dy + dz * dz + e2
            d2 = dx * dx + rho
            inv_d = lax.rsqrt(d2)
            inv = pl.reciprocal(rho, approx=True)
            inv = inv * (2.0 - rho * inv)
            normal_i = ci * dz - si * dy
            normal_j = ec2 * dz - es2 * dy
            planar = ci * ec + si * es
            amp = inv * (planar - normal_i * normal_j * inv) * (1.0 + dx * inv_d)
            lag = d2 * inv_d - dx
            for turn, (re, im) in zip(turns, stores):
                u = lag * turn
                u = u - ((u + ROUNDER) - ROUNDER)
                v = u * u
                re[at, lanes] = (amp * horner(v, COS_COEF)).astype(jnp.bfloat16)
                im[at, lanes] = (amp * u * horner(v, SIN_COEF)).astype(jnp.bfloat16)
        return carry

    lax.fori_loop(0, rows // ROWS, row_block, 0, unroll=4)


def dot(a, b):
    return jnp.dot(a, b, preferred_element_type=jnp.float32)


def product(kr, ks, pr, pi):
    return dot(kr, pr) + dot(ks, pi), dot(kr, pi) - dot(ks, pr)


def turns_of(recv_ref):
    return [recv_ref[:1, 5 + f : 6 + f] for f in range(2)]


def near_body(recv_ref, send0_ref, send1_ref, p0_ref, p1_ref, out_ref, k0_ref, k1_ref):
    freqs = range(p0_ref.shape[0])
    half = recv_ref.shape[0] // 2
    turns = turns_of(recv_ref)
    fill(recv_ref, send0_ref, turns, [(k0_ref.at[f, 0], k0_ref.at[f, 1]) for f in freqs])
    fill(recv_ref, send1_ref, turns, [(k1_ref.at[f, 0], k1_ref.at[f, 1]) for f in freqs])
    for f in freqs:
        for h in range(2):
            rows = slice(h * half, h * half + half)
            r0, i0 = product(k0_ref[f, 0, rows], k0_ref[f, 1, rows], p0_ref[f, 0], p0_ref[f, 1])
            r1, i1 = product(k1_ref[f, 0, rows], k1_ref[f, 1, rows], p1_ref[f, 0], p1_ref[f, 1])
            out_ref[f, 0, rows] = r0 + r1
            out_ref[f, 1, rows] = i0 + i1


def near(recv, send0, send1, p0, p1):
    freqs, _, boxes, width = p0.shape
    return pl.pallas_call(
        near_body,
        in_specs=[VMEM] * 5,
        out_specs=VMEM,
        out_shape=jax.ShapeDtypeStruct((freqs, 2, boxes, width), jnp.float32),
        scratch_shapes=[pltpu.VMEM((freqs, 2, boxes, boxes), jnp.bfloat16)] * 2,
        compiler_params=PARAMS,
        cost_estimate=cost(12),
    )(recv, send0, send1, p0, p1)


def choose(refs, rows):
    r = lax.rem(lax.axis_index("wide"), 4)
    inner = refs[1][rows]
    if len(refs) == 3:
        inner = jnp.where(r == 1, inner, refs[2][rows])
    return jnp.where(jnp.logical_or(r == 0, r == 3), refs[0][rows], inner)


def build_body(n_block, recv_ref, *rest):
    block_refs, kern_ref, send_ref = rest[:n_block], rest[-2], rest[-1]
    boxes = recv_ref.shape[0]
    send_ref[...] = unpack(choose(block_refs, slice(boxes, boxes + RECORD)))
    stores = [(kern_ref.at[f, 0], kern_ref.at[f, 1]) for f in range(kern_ref.shape[0])]
    fill(recv_ref, send_ref, turns_of(recv_ref), stores)


def build(recv, block, *after):
    boxes = recv.shape[0]
    return pl.pallas_call(
        functools.partial(build_body, len(block)),
        in_specs=[VMEM] * (1 + len(block)) + [ANY] * len(after),
        out_specs=VMEM,
        out_shape=jax.ShapeDtypeStruct((2, 2, boxes, boxes), jnp.bfloat16),
        scratch_shapes=[pltpu.VMEM((8, boxes), jnp.float32)],
        compiler_params=PARAMS,
        cost_estimate=cost(4),
    )(recv, *block, *after)


def part(kern_ref, f, p, which, rows):
    kr, ks = kern_ref[f, 0, rows], kern_ref[f, 1, rows]
    if which == 0:
        return dot(kr, p), -dot(ks, p)
    if which == 1:
        return dot(ks, p), dot(kr, p)
    boxes = p.shape[0] // 2
    return product(kr, ks, p[:boxes], p[boxes:])


def fold_body(f, which, n_blocks, n_acc, *refs):
    kern_refs, refs = refs[: len(n_blocks)], refs[len(n_blocks) :]
    blocks = []
    for n in n_blocks:
        blocks.append(refs[:n])
        refs = refs[n:]
    acc_refs, (out_ref, *p_refs) = refs[:n_acc], refs[-1 - len(n_blocks) :]
    boxes = kern_refs[0].shape[2]
    out = out_ref.at[0] if len(out_ref.shape) == 4 else out_ref
    for block, p_ref in zip(blocks, p_refs):
        p_ref[...] = choose(block, slice(0, p_ref.shape[0]))
    half = boxes // 2
    for h in range(2):
        rows = slice(h * half, h * half + half)
        acc = acc_refs[0].at[f] if len(acc_refs[0].shape) == 4 else acc_refs[0]
        re, im = acc[0, rows], acc[1, rows]
        for kern_ref, p_ref in zip(kern_refs, p_refs):
            more_re, more_im = part(kern_ref, f, p_ref[...], which, rows)
            re, im = re + more_re, im + more_im
        out[0, rows] = re
        out[1, rows] = im


def fold(f, which, kerns, blocks, accs, final=False):
    boxes, width = kerns[0].shape[2], blocks[0][0].shape[1]
    depth = boxes * (2 if which == 2 else 1)
    if final:
        out = jax.ShapeDtypeStruct((2, 2, boxes, width), jnp.float32)
        spec = pl.BlockSpec((1, 2, boxes, width), lambda i: (f, 0, 0, 0))
    else:
        out, spec = jax.ShapeDtypeStruct((2, boxes, width), jnp.float32), VMEM
    args = [*kerns, *[r for block in blocks for r in block], *accs]
    return pl.pallas_call(
        functools.partial(fold_body, f, which, [len(b) for b in blocks], len(accs)),
        grid=(1,),
        in_specs=[VMEM] * len(args),
        out_specs=spec,
        out_shape=out,
        scratch_shapes=[pltpu.VMEM((depth, width), jnp.bfloat16)] * len(blocks),
        compiler_params=PARAMS,
        cost_estimate=cost(2),
    )(*args)


def end_body(f, which, kern_ref, x_ref, y_ref, acc_ref, whole_ref, out_ref, p_ref):
    step = pl.program_id(0)
    tile = out_ref.shape[2]

    @pl.when(step == 0)
    def _():
        p_ref[...] = choose((x_ref, y_ref), slice(None))

    rows = pl.ds(pl.multiple_of(step * tile, tile), tile)
    re, im = part(kern_ref, f, p_ref[...], which, rows)
    out_ref[0, 0] = acc_ref[0, rows] + re
    out_ref[0, 1] = acc_ref[1, rows] + im


def end(f, which, kern, block, acc, out):
    depth, width = block[0].shape
    boxes = kern.shape[2]
    tile = boxes // 2
    return pl.pallas_call(
        functools.partial(end_body, f, which),
        grid=(2,),
        in_specs=[VMEM] * 4 + [ANY],
        out_specs=pl.BlockSpec((1, 2, tile, width), lambda i: (f, 0, i, 0)),
        out_shape=jax.ShapeDtypeStruct(out.shape, jnp.float32),
        scratch_shapes=[pltpu.VMEM((depth, width), jnp.bfloat16)],
        input_output_aliases={4: 0},
        compiler_params=PARAMS,
        cost_estimate=cost(2),
    )(kern, *block, acc, out)


def move(block, pairs):
    return lax.ppermute(block, "wide", pairs)


def routes(n):
    quads = range(0, n, 4)
    cross = [(b + r, b + (r ^ 2)) for b in quads for r in (0, 2)]
    cross += [(b + 3, (b + 7) % n) for b in quads] + [(b + 1, b + 1) for b in quads]
    spread = [
        p
        for b in quads
        for p in ((b + 1, b + 2), (b + 3, b + 1), (b, (b + 4) % n), ((b + 6) % n, b + 3))
    ]
    inner = [(b, b + 1) for b in quads]
    last = [p for b in quads for p in ((b + 1, b), (b + 2, b + 3))]
    pair = [(w, w ^ 1) for w in range(n)]
    return cross, spread, inner, last, pair


def ordered(value, *before):
    return lax.optimization_barrier((value, *before))[0]


def local(positions, spans, box_panel, panel_dihedral, freq_table, freq_index, pressures):
    n = lax.axis_size("wide")
    cross, spread, inner, last, pair = routes(n)
    _, _, boxes, width = pressures.shape
    send, recv, rows = prepare(
        positions, spans, box_panel, panel_dihedral, freq_table, freq_index
    )
    chunks = [
        jnp.concatenate([pressures[1, 0], rows], axis=0),
        pressures[0].reshape(2 * boxes, width),
        pressures[1, 1],
    ]
    crossed = [move(c, cross) for c in chunks]
    beside = move(pressures, pair)
    send1 = move(send, pair)
    base = near(recv, send, send1, pressures, beside)

    def onward(block):
        return move(block, spread), move(block, inner)

    first, second, base = lax.optimization_barrier((crossed[0], crossed[1], base))
    third, base = lax.optimization_barrier((crossed[2], base))
    spread0, inner0 = onward(first)
    spread1, inner1 = onward(second)
    spread2, inner2 = onward(third)
    spread0 = ordered(spread0, inner1, inner2)
    last0 = move(spread0, last)
    block0 = (spread0, inner0, first)
    kern_a = build(recv, block0)
    kern_b = build(recv, (last0, spread0))
    total = fold(1, 0, [kern_a, kern_b], [block0, (last0, spread0)], [base])
    spread1 = ordered(spread1, total)
    last1 = move(spread1, last)
    part0 = fold(0, 2, [kern_a], [(spread1, inner1, second)], [base])
    out = fold(0, 2, [kern_b], [(last1, spread1)], [part0], True)
    spread2 = ordered(spread2, out, total)
    last2 = move(spread2, last)
    total = fold(1, 1, [kern_a], [(spread2, inner2, third)], [total])
    return end(1, 1, kern_b, (last2, spread2), total, out)


def solution(mesh):
    placed = (
        P(None, "wide"),
        P("wide"),
        P("wide"),
        P(),
        P(),
        P("groups"),
        P("groups", None, "wide", None),
    )
    return jax.shard_map(
        local,
        mesh=mesh,
        in_specs=placed,
        out_specs=P("groups", None, "wide", None),
        check_vma=False,
    )
```

```python
import functools

import jax
import jax.numpy as jnp
from jax import lax
from jax.experimental import pallas as pl
from jax.experimental.pallas import tpu as pltpu
from jax.sharding import PartitionSpec as P

SIN_COEF = (6.283182621002197, -41.3414192199707, 81.5961685180664, -76.5799560546875, 41.20474624633789, -12.27022647857666)
COS_COEF = (0.9999992251396179, -19.738981246948242, 64.9287109375, -85.27218627929688, 58.7929573059082, -21.074859619140625)
ROUNDER = 12582912.0
TURN = 0.15915494309189535
ROWS = 32
LANES = 128
RECORD = 32
VMEM = pl.BlockSpec(memory_space=pltpu.VMEM)
ANY = pl.BlockSpec(memory_space=pl.ANY)
PARAMS = pltpu.CompilerParams(vmem_limit_bytes=24 * 1024 * 1024)


def horner(v, coef):
    value = coef[-1] * v + coef[-2]
    for c in coef[-3::-1]:
        value = value * v + c
    return value


def cost(micros):
    return pl.CostEstimate(flops=micros << 33, bytes_accessed=1, transcendentals=0)


def prep_body(
    pos_any, span_any, panel_any, dihedral_any, table_any, index_any,
    send_ref, recv_ref, rows_ref,
    pos_ref, span_ref, panel_ref, dihedral_ref, table_ref, index_ref, sems
):
    boxes = pos_ref.shape[1]
    copies = [
        pltpu.make_async_copy(src, dst, sems.at[i])
        for i, (src, dst) in enumerate(
            [(pos_any, pos_ref), (span_any, span_ref), (panel_any, panel_ref)]
            + [(dihedral_any, dihedral_ref), (table_any, table_ref), (index_any, index_ref)]
        )
    ]
    for copy in copies:
        copy.start()
    for copy in copies:
        copy.wait()
    panel = panel_ref[...].reshape(1, boxes)
    angle = jnp.zeros(panel.shape, jnp.float32)
    for i in range(dihedral_ref.shape[0]):
        angle = jnp.where(panel == i, dihedral_ref[i], angle)
    sin, cos, span = jnp.sin(angle), jnp.cos(angle), span_ref[...].reshape(1, boxes)
    pos = pos_ref[...]
    send = jnp.concatenate(
        [pos, span * span, 2.0 * span * sin, 2.0 * span * cos, span * sin, span * cos], axis=0
    )
    send_ref[...] = send
    turns = [jnp.full_like(sin, table_ref[index_ref[f]] * TURN) for f in range(index_ref.shape[0])]
    recv_ref[...] = jnp.concatenate([pos, sin, cos, *turns, sin], axis=0).T
    high = send.astype(jnp.bfloat16).astype(jnp.float32)
    left = send - high
    middle = left.astype(jnp.bfloat16).astype(jnp.float32)
    rows_ref[...] = jnp.concatenate(
        [high, middle, left - middle, jnp.zeros_like(high)], axis=0
    ).astype(jnp.bfloat16)


def prepare(positions, spans, box_panel, panel_dihedral, freq_table, freq_index):
    args = (positions, spans, box_panel, panel_dihedral, freq_table, freq_index)
    boxes = spans.shape[0]
    return pl.pallas_call(
        prep_body,
        in_specs=[pl.BlockSpec(memory_space=pltpu.HBM)] * 6,
        out_specs=[VMEM] * 3,
        out_shape=[
            jax.ShapeDtypeStruct((8, boxes), jnp.float32),
            jax.ShapeDtypeStruct((boxes, 8), jnp.float32),
            jax.ShapeDtypeStruct((RECORD, boxes), jnp.bfloat16),
        ],
        scratch_shapes=[
            pltpu.VMEM(positions.shape, jnp.float32),
            pltpu.VMEM(spans.shape, jnp.float32),
            pltpu.VMEM(box_panel.shape, jnp.int32),
            pltpu.SMEM(panel_dihedral.shape, jnp.float32),
            pltpu.SMEM(freq_table.shape, jnp.float32),
            pltpu.SMEM(freq_index.shape, jnp.int32),
            pltpu.SemaphoreType.DMA((6,)),
        ],
        compiler_params=PARAMS,
        cost_estimate=cost(2),
    )(*[pltpu.with_memory_space_constraint(a, pltpu.HBM) for a in args])


def unpack(rows):
    parts = rows.astype(jnp.float32)
    return (parts[:8] + parts[8:16]) + parts[16:24]


def fill(recv_ref, send_ref, turns, stores):
    rows, boxes = recv_ref.shape[0], send_ref.shape[1]

    def row_block(i, carry):
        at = pl.ds(pl.multiple_of(i * ROWS, ROWS), ROWS)
        xi, yi, zi, si, ci = [
            jnp.broadcast_to(recv_ref[at, q : q + 1], (ROWS, LANES)) for q in range(5)
        ]
        for j in range(boxes // LANES):
            lanes = pl.ds(j * LANES, LANES)
            xj, yj, zj, e2, es2, ec2, es, ec = [send_ref[q : q + 1, lanes] for q in range(8)]
            dx, dy, dz = xi - xj, yi - yj, zi - zj
            rho = dy * dy + dz * dz + e2
            d2 = dx * dx + rho
            inv_d = lax.rsqrt(d2)
            inv = lax.rsqrt(rho)
            inv = inv * inv
            normal_i = ci * dz - si * dy
            normal_j = ec2 * dz - es2 * dy
            planar = ci * ec + si * es
            amp = inv * (planar - normal_i * normal_j * inv) * (1.0 + dx * inv_d)
            lag = d2 * inv_d - dx
            for turn, (re, im) in zip(turns, stores):
                u = lag * turn
                u = u - ((u + ROUNDER) - ROUNDER)
                v = u * u
                re[at, lanes] = (amp * horner(v, COS_COEF)).astype(jnp.bfloat16)
                im[at, lanes] = (amp * u * horner(v, SIN_COEF)).astype(jnp.bfloat16)
        return carry

    lax.fori_loop(0, rows // ROWS, row_block, 0, unroll=4)


def dot(a, b):
    return jnp.dot(a, b, preferred_element_type=jnp.float32)


def product(kr, ks, pr, pi):
    return dot(kr, pr) + dot(ks, pi), dot(kr, pi) - dot(ks, pr)


def turns_of(recv_ref):
    return [recv_ref[:1, 5 + f : 6 + f] for f in range(2)]


def near_body(recv_ref, send0_ref, send1_ref, p0_ref, p1_ref, out_ref, k0_ref, k1_ref):
    freqs = range(p0_ref.shape[0])
    half = recv_ref.shape[0] // 2
    turns = turns_of(recv_ref)
    fill(recv_ref, send0_ref, turns, [(k0_ref.at[f, 0], k0_ref.at[f, 1]) for f in freqs])
    fill(recv_ref, send1_ref, turns, [(k1_ref.at[f, 0], k1_ref.at[f, 1]) for f in freqs])
    for f in freqs:
        for h in range(2):
            rows = slice(h * half, h * half + half)
            r0, i0 = product(k0_ref[f, 0, rows], k0_ref[f, 1, rows], p0_ref[f, 0], p0_ref[f, 1])
            r1, i1 = product(k1_ref[f, 0, rows], k1_ref[f, 1, rows], p1_ref[f, 0], p1_ref[f, 1])
            out_ref[f, 0, rows] = r0 + r1
            out_ref[f, 1, rows] = i0 + i1


def near(recv, send0, send1, p0, p1):
    freqs, _, boxes, width = p0.shape
    return pl.pallas_call(
        near_body,
        in_specs=[VMEM] * 5,
        out_specs=VMEM,
        out_shape=jax.ShapeDtypeStruct((freqs, 2, boxes, width), jnp.float32),
        scratch_shapes=[pltpu.VMEM((freqs, 2, boxes, boxes), jnp.bfloat16)] * 2,
        compiler_params=PARAMS,
        cost_estimate=cost(12),
    )(recv, send0, send1, p0, p1)


def choose(refs, rows):
    r = lax.rem(lax.axis_index("wide"), 4)
    inner = refs[1][rows]
    if len(refs) == 3:
        inner = jnp.where(r == 1, inner, refs[2][rows])
    return jnp.where(jnp.logical_or(r == 0, r == 3), refs[0][rows], inner)


def build_body(n_block, recv_ref, *rest):
    block_refs, kern_ref, send_ref = rest[:n_block], rest[-2], rest[-1]
    boxes = recv_ref.shape[0]
    send_ref[...] = unpack(choose(block_refs, slice(boxes, boxes + RECORD)))
    stores = [(kern_ref.at[f, 0], kern_ref.at[f, 1]) for f in range(kern_ref.shape[0])]
    fill(recv_ref, send_ref, turns_of(recv_ref), stores)


def build(recv, block, *after):
    boxes = recv.shape[0]
    return pl.pallas_call(
        functools.partial(build_body, len(block)),
        in_specs=[VMEM] * (1 + len(block)) + [ANY] * len(after),
        out_specs=VMEM,
        out_shape=jax.ShapeDtypeStruct((2, 2, boxes, boxes), jnp.bfloat16),
        scratch_shapes=[pltpu.VMEM((8, boxes), jnp.float32)],
        compiler_params=PARAMS,
        cost_estimate=cost(4),
    )(recv, *block, *after)


def part(kern_ref, f, p, which, rows):
    kr, ks = kern_ref[f, 0, rows], kern_ref[f, 1, rows]
    if which == 0:
        return dot(kr, p), -dot(ks, p)
    if which == 1:
        return dot(ks, p), dot(kr, p)
    boxes = p.shape[0] // 2
    return product(kr, ks, p[:boxes], p[boxes:])


def fold_body(f, which, n_blocks, *refs):
    kern_refs, refs = refs[: len(n_blocks)], refs[len(n_blocks) :]
    blocks = []
    for n in n_blocks:
        blocks.append(refs[:n])
        refs = refs[n:]
    acc_ref, (out_ref, *p_refs) = refs[0], refs[-1 - len(n_blocks) :]
    boxes = kern_refs[0].shape[2]
    for block, p_ref in zip(blocks, p_refs):
        p_ref[...] = choose(block, slice(0, p_ref.shape[0]))
    half = boxes // 2
    for h in range(2):
        rows = slice(h * half, h * half + half)
        acc = acc_ref.at[f] if len(acc_ref.shape) == 4 else acc_ref
        re, im = acc[0, rows], acc[1, rows]
        for kern_ref, p_ref in zip(kern_refs, p_refs):
            more_re, more_im = part(kern_ref, f, p_ref[...], which, rows)
            re, im = re + more_re, im + more_im
        out_ref[0, rows] = re
        out_ref[1, rows] = im


def fold(f, which, kerns, blocks, acc):
    boxes, width = kerns[0].shape[2], blocks[0][0].shape[1]
    depth = boxes * (2 if which == 2 else 1)
    args = [*kerns, *[r for block in blocks for r in block], acc]
    return pl.pallas_call(
        functools.partial(fold_body, f, which, [len(b) for b in blocks]),
        in_specs=[VMEM] * len(args),
        out_specs=VMEM,
        out_shape=jax.ShapeDtypeStruct((2, boxes, width), jnp.float32),
        scratch_shapes=[pltpu.VMEM((depth, width), jnp.bfloat16)] * len(blocks),
        compiler_params=PARAMS,
        cost_estimate=cost(2),
    )(*args)


def end_body(f, which, kern_ref, x_ref, y_ref, acc_ref, *rest):
    out_ref, p_ref = rest[-2:]
    step = pl.program_id(0)
    tile = out_ref.shape[2]

    @pl.when(step == 0)
    def _():
        p_ref[...] = choose((x_ref, y_ref), slice(None))

    rows = pl.ds(pl.multiple_of(step * tile, tile), tile)
    re, im = part(kern_ref, f, p_ref[...], which, rows)
    out_ref[0, 0] = acc_ref[0, rows] + re
    out_ref[0, 1] = acc_ref[1, rows] + im


def end(f, which, kern, block, acc, *out):
    depth, width = block[0].shape
    boxes = kern.shape[2]
    tile = boxes // 2
    return pl.pallas_call(
        functools.partial(end_body, f, which),
        grid=(2,),
        in_specs=[VMEM] * 4 + [ANY] * len(out),
        out_specs=pl.BlockSpec((1, 2, tile, width), lambda i: (f, 0, i, 0)),
        out_shape=jax.ShapeDtypeStruct((2, 2, boxes, width), jnp.float32),
        scratch_shapes=[pltpu.VMEM((depth, width), jnp.bfloat16)],
        input_output_aliases={4: 0} if out else {},
        compiler_params=PARAMS,
        cost_estimate=cost(2),
    )(kern, *block, acc, *out)


def move(block, pairs):
    return lax.ppermute(block, "wide", pairs)


def routes(n):
    quads = range(0, n, 4)
    cross = [(b + r, b + (r ^ 2)) for b in quads for r in (0, 2)]
    cross += [(b + 3, (b + 7) % n) for b in quads] + [(b + 1, b + 1) for b in quads]
    spread = [
        p
        for b in quads
        for p in ((b + 1, b + 2), (b + 3, b + 1), (b, (b + 4) % n), ((b + 6) % n, b + 3))
    ]
    inner = [(b, b + 1) for b in quads]
    last = [p for b in quads for p in ((b + 1, b), (b + 2, b + 3))]
    pair = [(w, w ^ 1) for w in range(n)]
    return cross, spread, inner, last, pair


def ordered(value, *before):
    return lax.optimization_barrier((value, *before))[0]


def local(positions, spans, box_panel, panel_dihedral, freq_table, freq_index, pressures):
    n = lax.axis_size("wide")
    cross, spread, inner, last, pair = routes(n)
    _, _, boxes, width = pressures.shape
    send, recv, rows = prepare(
        positions, spans, box_panel, panel_dihedral, freq_table, freq_index
    )
    chunks = [
        jnp.concatenate([pressures[1, 0], rows], axis=0),
        pressures[0].reshape(2 * boxes, width),
        pressures[1, 1],
    ]
    crossed = [move(c, cross) for c in chunks]
    beside = move(pressures, pair)
    send1 = move(send, pair)
    base = near(recv, send, send1, pressures, beside)

    def onward(block):
        return move(block, spread), move(block, inner)

    first, second, base = lax.optimization_barrier((crossed[0], crossed[1], base))
    third, base = lax.optimization_barrier((crossed[2], base))
    spread0, inner0 = onward(first)
    spread1 = move(second, spread)
    spread2, inner2 = onward(third)
    inner1 = move(second, inner)
    spread0 = ordered(spread0, inner1, inner2)
    last0 = move(spread0, last)
    block0 = (spread0, inner0, first)
    kern_a = build(recv, block0)
    kern_b = build(recv, (last0, spread0))
    total = fold(1, 0, [kern_a, kern_b], [block0, (last0, spread0)], base)
    spread2 = ordered(spread2, total)
    last2 = move(spread2, last)
    total = fold(1, 1, [kern_a], [(spread2, inner2, third)], total)
    out = end(1, 1, kern_b, (last2, spread2), total)
    spread1 = ordered(spread1, out)
    last1 = move(spread1, last)
    part0 = fold(0, 2, [kern_a], [(spread1, inner1, second)], base)
    return end(0, 2, kern_b, (last1, spread1), part0, out)


def solution(mesh):
    placed = (
        P(None, "wide"),
        P("wide"),
        P("wide"),
        P(),
        P(),
        P("groups"),
        P("groups", None, "wide", None),
    )
    return jax.shard_map(
        local,
        mesh=mesh,
        in_specs=placed,
        out_specs=P("groups", None, "wide", None),
        check_vma=False,
    )
```

```python
import functools

import jax
import jax.numpy as jnp
from jax import lax
from jax.experimental import pallas as pl
from jax.experimental.pallas import tpu as pltpu
from jax.sharding import PartitionSpec as P

SIN_COEF = (6.283182621002197, -41.3414192199707, 81.5961685180664, -76.5799560546875, 41.20474624633789, -12.27022647857666)
COS_COEF = (0.9999992251396179, -19.738981246948242, 64.9287109375, -85.27218627929688, 58.7929573059082, -21.074859619140625)
ROUNDER = 12582912.0
TURN = 0.15915494309189535
ROWS = 32
LANES = 128
RECORD = 32
VMEM = pl.BlockSpec(memory_space=pltpu.VMEM)
ANY = pl.BlockSpec(memory_space=pl.ANY)
PARAMS = pltpu.CompilerParams(vmem_limit_bytes=24 * 1024 * 1024)


def horner(v, coef):
    value = coef[-1] * v + coef[-2]
    for c in coef[-3::-1]:
        value = value * v + c
    return value


def cost(micros):
    return pl.CostEstimate(flops=micros << 33, bytes_accessed=1, transcendentals=0)


def prep_body(
    pos_any, span_any, panel_any, dihedral_any, table_any, index_any,
    send_ref, recv_ref, rows_ref,
    pos_ref, span_ref, panel_ref, dihedral_ref, table_ref, index_ref, sems
):
    boxes = pos_ref.shape[1]
    copies = [
        pltpu.make_async_copy(src, dst, sems.at[i])
        for i, (src, dst) in enumerate(
            [(pos_any, pos_ref), (span_any, span_ref), (panel_any, panel_ref)]
            + [(dihedral_any, dihedral_ref), (table_any, table_ref), (index_any, index_ref)]
        )
    ]
    for copy in copies:
        copy.start()
    for copy in copies:
        copy.wait()
    panel = panel_ref[...].reshape(1, boxes)
    angle = jnp.zeros(panel.shape, jnp.float32)
    for i in range(dihedral_ref.shape[0]):
        angle = jnp.where(panel == i, dihedral_ref[i], angle)
    sin, cos, span = jnp.sin(angle), jnp.cos(angle), span_ref[...].reshape(1, boxes)
    pos = pos_ref[...]
    send = jnp.concatenate(
        [pos, span * span, 2.0 * span * sin, 2.0 * span * cos, span * sin, span * cos], axis=0
    )
    send_ref[...] = send
    turns = [jnp.full_like(sin, table_ref[index_ref[f]] * TURN) for f in range(index_ref.shape[0])]
    recv_ref[...] = jnp.concatenate([pos, sin, cos, *turns, sin], axis=0).T
    high = send.astype(jnp.bfloat16).astype(jnp.float32)
    left = send - high
    middle = left.astype(jnp.bfloat16).astype(jnp.float32)
    rows_ref[...] = jnp.concatenate(
        [high, middle, left - middle, jnp.zeros_like(high)], axis=0
    ).astype(jnp.bfloat16)


def prepare(positions, spans, box_panel, panel_dihedral, freq_table, freq_index):
    args = (positions, spans, box_panel, panel_dihedral, freq_table, freq_index)
    boxes = spans.shape[0]
    return pl.pallas_call(
        prep_body,
        in_specs=[pl.BlockSpec(memory_space=pltpu.HBM)] * 6,
        out_specs=[VMEM] * 3,
        out_shape=[
            jax.ShapeDtypeStruct((8, boxes), jnp.float32),
            jax.ShapeDtypeStruct((boxes, 8), jnp.float32),
            jax.ShapeDtypeStruct((RECORD, boxes), jnp.bfloat16),
        ],
        scratch_shapes=[
            pltpu.VMEM(positions.shape, jnp.float32),
            pltpu.VMEM(spans.shape, jnp.float32),
            pltpu.VMEM(box_panel.shape, jnp.int32),
            pltpu.SMEM(panel_dihedral.shape, jnp.float32),
            pltpu.SMEM(freq_table.shape, jnp.float32),
            pltpu.SMEM(freq_index.shape, jnp.int32),
            pltpu.SemaphoreType.DMA((6,)),
        ],
        compiler_params=PARAMS,
        cost_estimate=cost(2),
    )(*[pltpu.with_memory_space_constraint(a, pltpu.HBM) for a in args])


def unpack(rows):
    parts = rows.astype(jnp.float32)
    return (parts[:8] + parts[8:16]) + parts[16:24]


def fill(recv_ref, send_ref, turns, stores):
    rows, boxes = recv_ref.shape[0], send_ref.shape[1]

    def row_block(i, carry):
        at = pl.ds(pl.multiple_of(i * ROWS, ROWS), ROWS)
        xi, yi, zi, si, ci = [
            jnp.broadcast_to(recv_ref[at, q : q + 1], (ROWS, LANES)) for q in range(5)
        ]
        for j in range(boxes // LANES):
            lanes = pl.ds(j * LANES, LANES)
            xj, yj, zj, e2, es2, ec2, es, ec = [send_ref[q : q + 1, lanes] for q in range(8)]
            dx, dy, dz = xi - xj, yi - yj, zi - zj
            rho = dy * dy + dz * dz + e2
            d2 = dx * dx + rho
            inv_d = lax.rsqrt(d2)
            inv = lax.rsqrt(rho)
            inv = inv * inv
            normal_i = ci * dz - si * dy
            normal_j = ec2 * dz - es2 * dy
            planar = ci * ec + si * es
            amp = inv * (planar - normal_i * normal_j * inv) * (1.0 + dx * inv_d)
            lag = d2 * inv_d - dx
            for turn, (re, im) in zip(turns, stores):
                u = lag * turn
                u = u - ((u + ROUNDER) - ROUNDER)
                v = u * u
                re[at, lanes] = (amp * horner(v, COS_COEF)).astype(jnp.bfloat16)
                im[at, lanes] = (amp * u * horner(v, SIN_COEF)).astype(jnp.bfloat16)
        return carry

    lax.fori_loop(0, rows // ROWS, row_block, 0, unroll=8)


def dot(a, b):
    return jnp.dot(a, b, preferred_element_type=jnp.float32)


def product(kr, ks, pr, pi):
    return dot(kr, pr) + dot(ks, pi), dot(kr, pi) - dot(ks, pr)


def turns_of(recv_ref):
    return [recv_ref[:1, 5 + f : 6 + f] for f in range(2)]


def near_body(recv_ref, send0_ref, send1_ref, p0_ref, p1_ref, out_ref, k0_ref, k1_ref):
    freqs = range(p0_ref.shape[0])
    half = recv_ref.shape[0] // 2
    turns = turns_of(recv_ref)
    fill(recv_ref, send0_ref, turns, [(k0_ref.at[f, 0], k0_ref.at[f, 1]) for f in freqs])
    fill(recv_ref, send1_ref, turns, [(k1_ref.at[f, 0], k1_ref.at[f, 1]) for f in freqs])
    for f in freqs:
        for h in range(2):
            rows = slice(h * half, h * half + half)
            r0, i0 = product(k0_ref[f, 0, rows], k0_ref[f, 1, rows], p0_ref[f, 0], p0_ref[f, 1])
            r1, i1 = product(k1_ref[f, 0, rows], k1_ref[f, 1, rows], p1_ref[f, 0], p1_ref[f, 1])
            out_ref[f, 0, rows] = r0 + r1
            out_ref[f, 1, rows] = i0 + i1


def near(recv, send0, send1, p0, p1):
    freqs, _, boxes, width = p0.shape
    return pl.pallas_call(
        near_body,
        in_specs=[VMEM] * 5,
        out_specs=VMEM,
        out_shape=jax.ShapeDtypeStruct((freqs, 2, boxes, width), jnp.float32),
        scratch_shapes=[pltpu.VMEM((freqs, 2, boxes, boxes), jnp.bfloat16)] * 2,
        compiler_params=PARAMS,
        cost_estimate=cost(12),
    )(recv, send0, send1, p0, p1)


def choose(refs, rows):
    r = lax.rem(lax.axis_index("wide"), 4)
    inner = refs[1][rows]
    if len(refs) == 3:
        inner = jnp.where(r == 1, inner, refs[2][rows])
    return jnp.where(jnp.logical_or(r == 0, r == 3), refs[0][rows], inner)


def build_body(n_block, recv_ref, *rest):
    block_refs, kern_ref, send_ref = rest[:n_block], rest[-2], rest[-1]
    boxes = recv_ref.shape[0]
    send_ref[...] = unpack(choose(block_refs, slice(boxes, boxes + RECORD)))
    stores = [(kern_ref.at[f, 0], kern_ref.at[f, 1]) for f in range(kern_ref.shape[0])]
    fill(recv_ref, send_ref, turns_of(recv_ref), stores)


def build(recv, block, *after):
    boxes = recv.shape[0]
    return pl.pallas_call(
        functools.partial(build_body, len(block)),
        in_specs=[VMEM] * (1 + len(block)) + [ANY] * len(after),
        out_specs=VMEM,
        out_shape=jax.ShapeDtypeStruct((2, 2, boxes, boxes), jnp.bfloat16),
        scratch_shapes=[pltpu.VMEM((8, boxes), jnp.float32)],
        compiler_params=PARAMS,
        cost_estimate=cost(4),
    )(recv, *block, *after)


def part(kern_ref, f, p, which, rows):
    kr, ks = kern_ref[f, 0, rows], kern_ref[f, 1, rows]
    if which == 0:
        return dot(kr, p), -dot(ks, p)
    if which == 1:
        return dot(ks, p), dot(kr, p)
    boxes = p.shape[0] // 2
    return product(kr, ks, p[:boxes], p[boxes:])


def fold_body(f, which, n_blocks, n_acc, *refs):
    kern_refs, refs = refs[: len(n_blocks)], refs[len(n_blocks) :]
    blocks = []
    for n in n_blocks:
        blocks.append(refs[:n])
        refs = refs[n:]
    acc_refs, (out_ref, *p_refs) = refs[:n_acc], refs[-1 - len(n_blocks) :]
    boxes = kern_refs[0].shape[2]
    out = out_ref.at[0] if len(out_ref.shape) == 4 else out_ref
    for block, p_ref in zip(blocks, p_refs):
        p_ref[...] = choose(block, slice(0, p_ref.shape[0]))
    half = boxes // 2
    for h in range(2):
        rows = slice(h * half, h * half + half)
        acc = acc_refs[0].at[f] if len(acc_refs[0].shape) == 4 else acc_refs[0]
        re, im = acc[0, rows], acc[1, rows]
        for kern_ref, p_ref in zip(kern_refs, p_refs):
            more_re, more_im = part(kern_ref, f, p_ref[...], which, rows)
            re, im = re + more_re, im + more_im
        out[0, rows] = re
        out[1, rows] = im


def fold(f, which, kerns, blocks, accs, final=False):
    boxes, width = kerns[0].shape[2], blocks[0][0].shape[1]
    depth = boxes * (2 if which == 2 else 1)
    if final:
        out = jax.ShapeDtypeStruct((2, 2, boxes, width), jnp.float32)
        spec = pl.BlockSpec((1, 2, boxes, width), lambda i: (f, 0, 0, 0))
    else:
        out, spec = jax.ShapeDtypeStruct((2, boxes, width), jnp.float32), VMEM
    args = [*kerns, *[r for block in blocks for r in block], *accs]
    return pl.pallas_call(
        functools.partial(fold_body, f, which, [len(b) for b in blocks], len(accs)),
        grid=(1,),
        in_specs=[VMEM] * len(args),
        out_specs=spec,
        out_shape=out,
        scratch_shapes=[pltpu.VMEM((depth, width), jnp.bfloat16)] * len(blocks),
        compiler_params=PARAMS,
        cost_estimate=cost(2),
    )(*args)


def end_body(f, which, kern_ref, x_ref, y_ref, acc_ref, whole_ref, out_ref, p_ref):
    step = pl.program_id(0)
    tile = out_ref.shape[2]

    @pl.when(step == 0)
    def _():
        p_ref[...] = choose((x_ref, y_ref), slice(None))

    rows = pl.ds(pl.multiple_of(step * tile, tile), tile)
    re, im = part(kern_ref, f, p_ref[...], which, rows)
    out_ref[0, 0] = acc_ref[0, rows] + re
    out_ref[0, 1] = acc_ref[1, rows] + im


def end(f, which, kern, block, acc, out):
    depth, width = block[0].shape
    boxes = kern.shape[2]
    tile = boxes // 2
    return pl.pallas_call(
        functools.partial(end_body, f, which),
        grid=(2,),
        in_specs=[VMEM] * 4 + [ANY],
        out_specs=pl.BlockSpec((1, 2, tile, width), lambda i: (f, 0, i, 0)),
        out_shape=jax.ShapeDtypeStruct(out.shape, jnp.float32),
        scratch_shapes=[pltpu.VMEM((depth, width), jnp.bfloat16)],
        input_output_aliases={4: 0},
        compiler_params=PARAMS,
        cost_estimate=cost(2),
    )(kern, *block, acc, out)


def move(block, pairs):
    return lax.ppermute(block, "wide", pairs)


def routes(n):
    quads = range(0, n, 4)
    cross = [(b + r, b + (r ^ 2)) for b in quads for r in (0, 2)]
    cross += [(b + 3, (b + 7) % n) for b in quads] + [(b + 1, b + 1) for b in quads]
    spread = [
        p
        for b in quads
        for p in ((b + 1, b + 2), (b + 3, b + 1), (b, (b + 4) % n), ((b + 6) % n, b + 3))
    ]
    inner = [(b, b + 1) for b in quads]
    last = [p for b in quads for p in ((b + 1, b), (b + 2, b + 3))]
    pair = [(w, w ^ 1) for w in range(n)]
    return cross, spread, inner, last, pair


def ordered(value, *before):
    return lax.optimization_barrier((value, *before))[0]


def local(positions, spans, box_panel, panel_dihedral, freq_table, freq_index, pressures):
    n = lax.axis_size("wide")
    cross, spread, inner, last, pair = routes(n)
    _, _, boxes, width = pressures.shape
    send, recv, rows = prepare(
        positions, spans, box_panel, panel_dihedral, freq_table, freq_index
    )
    chunks = [
        jnp.concatenate([pressures[1, 0], rows], axis=0),
        pressures[0].reshape(2 * boxes, width),
        pressures[1, 1],
    ]
    crossed = [move(c, cross) for c in chunks]
    beside = move(pressures, pair)
    send1 = move(send, pair)
    base = near(recv, send, send1, pressures, beside)

    def onward(block):
        return move(block, spread), move(block, inner)

    first, second, base = lax.optimization_barrier((crossed[0], crossed[1], base))
    third, base = lax.optimization_barrier((crossed[2], base))
    spread0, inner0 = onward(first)
    spread1, inner1 = onward(second)
    spread2, inner2 = onward(third)
    spread0 = ordered(spread0, inner1, inner2)
    last0 = move(spread0, last)
    block0 = (spread0, inner0, first)
    kern_a = build(recv, block0)
    kern_b = build(recv, (last0, spread0))
    total = fold(1, 0, [kern_a, kern_b], [block0, (last0, spread0)], [base])
    spread1 = ordered(spread1, total)
    last1 = move(spread1, last)
    part0 = fold(0, 2, [kern_a], [(spread1, inner1, second)], [base])
    out = fold(0, 2, [kern_b], [(last1, spread1)], [part0], True)
    spread2 = ordered(spread2, out, total)
    last2 = move(spread2, last)
    total = fold(1, 1, [kern_a], [(spread2, inner2, third)], [total])
    return end(1, 1, kern_b, (last2, spread2), total, out)


def solution(mesh):
    placed = (
        P(None, "wide"),
        P("wide"),
        P("wide"),
        P(),
        P(),
        P("groups"),
        P("groups", None, "wide", None),
    )
    return jax.shard_map(
        local,
        mesh=mesh,
        in_specs=placed,
        out_specs=P("groups", None, "wide", None),
        check_vma=False,
    )
```
